32 devices in a mesh: particle: 4 (over z), field: 8 (over y, x, core).
Axes of the slice: x: 2, y: 2, z: 4, core: 2. Of those that a mesh axis runs over, the one named last changes fastest.
Arguments:
- vorticity: bfloat16 [4, 1024, 1024], P('particle', 'field'), may hold values from -6 to 6
- ancestors: int32 [4], replicated, may hold values from 0 to 3
- noise: bfloat16 [4, 1024, 1024], P('particle', 'field'), may hold values from -6 to 6
Outputs:
- forecast: float32 [4, 1024, 1024], P('particle', 'field')
The draws below stay inside these ranges and needn't reach their ends.
All inputs are finite; a program needn't handle non-finite values.
Results may differ from the reference program's by a relative error of at most 0.0003.
Values may be sent and summed in bfloat16 or wider, within the bound.
A program may use at most 64 MiB of HBM per device.

```python
import math
import jax
import jax.numpy as jnp
import numpy as np
from jax import lax

GRID = 1024
PARTICLES = 4


def set_ends(drawn, rng, low, largest):
    extent = drawn.shape
    spot = [jax.random.randint(jax.random.fold_in(rng, axis), (), 0, extent[axis]) for axis in range(len(extent))]
    drawn = drawn.at[tuple(spot)].set(low)
    longest = extent.index(max(extent))
    spot[longest] = (spot[longest] + 1) % extent[longest]
    return drawn.at[tuple(spot)].set(largest)


def block_scale(own_key, extent, shards, least, largest):
    factor_of, own = 1.0, jax.random.fold_in(own_key, 6)
    for dim, shards_of in shards:
        steps = jnp.exp(jax.random.uniform(jax.random.fold_in(own, dim), (shards_of,), jnp.float32, least / len(shards), largest / len(shards)))
        factor_of = factor_of * jnp.repeat(steps, extent[dim] // shards_of).reshape([-1 if axis == dim else 1 for axis in range(len(extent))])
    return factor_of


def rank_bounds(count, lean):
    loads = [(1 << 20) // math.isqrt(standing ** lean) + 1 for standing in range(1, count + 1)]
    spread = 1 + sum(loads) // (1 << 30)
    return np.cumsum(np.array([max(1, weight // spread) for weight in loads]))


def skewed_ids(own_key, shape, number_of, skew):
    listing = rank_bounds(number_of, skew)
    lot = jax.random.randint(jax.random.fold_in(own_key, 1), shape, 0, int(listing[number_of - 1]))
    grade = jnp.searchsorted(jnp.asarray(listing, jnp.int32), lot, side="right")
    return jax.random.permutation(jax.random.fold_in(own_key, 2), number_of)[grade].astype(jnp.int32)


def normal_values(own_key, dims, deviation, most, shards=(), kind=jnp.bfloat16):
    array = deviation * jax.random.normal(own_key, dims, jnp.float32)
    if shards:
        array = array * block_scale(own_key, dims, shards, -0.22, 0.18)
    return jnp.clip(array, -most, most).astype(kind)


def setup_inputs(seed: int = 0) -> dict:
    streams_of = jax.random.split(jax.random.key(seed), 4)
    vorticity = normal_values(streams_of[0], (PARTICLES, GRID, GRID), 1.0, 6.0, ((0, 4), (1, 8)))
    ancestors = set_ends(skewed_ids(streams_of[1], (PARTICLES,), PARTICLES, 2), jax.random.fold_in(streams_of[1], 3), 0, PARTICLES - 1).astype(jnp.int32)
    noise = normal_values(streams_of[2], (PARTICLES, GRID, GRID), 1.0, 6.0, ((0, 4), (1, 8)))
    return dict(vorticity=vorticity, ancestors=ancestors, noise=noise)


PARENT_WEIGHT = 0.8
NOISE_WEIGHT = 0.6
VISCOSITY = 0.05
TIME_STEP = 0.1


def wave_tables(modes, length):
    signed = jnp.where(modes >= length // 2, modes - length, modes)
    wavenumber = (2.0 * math.pi / length) * signed.astype(jnp.float32)
    slope = jnp.where(modes == length // 2, jnp.zeros_like(wavenumber), wavenumber)
    retained = jnp.where(3 * jnp.abs(signed) < length, 1.0, 0.0).astype(jnp.float32)
    return wavenumber, slope, retained


def reference(vorticity, ancestors, noise):
    length = vorticity.shape[-1]
    wavenumber, slope, retained = wave_tables(jnp.arange(length, dtype=jnp.int32), length)
    squared = wavenumber[:, None] ** 2 + wavenumber[None, :] ** 2
    inverse_sq = jnp.where(squared > 0, 1.0 / jnp.where(squared > 0, squared, 1.0), 0.0)
    dealias = retained[:, None] * retained[None, :]
    spectrum_weight = 1.0 / (1.0 + squared)
    slope_x = slope[None, :]
    slope_y = slope[:, None]

    def tendency(spectral):
        potential = spectral * inverse_sq
        speed_x = jnp.fft.ifft2(1j * slope_y * potential).real
        speed_y = jnp.fft.ifft2(-1j * slope_x * potential).real
        grad_x = jnp.fft.ifft2(1j * slope_x * spectral).real
        grad_y = jnp.fft.ifft2(1j * slope_y * spectral).real
        advection = speed_x * grad_x + speed_y * grad_y
        return -dealias * jnp.fft.fft2(advection) - VISCOSITY * squared * spectral

    def propose_one(item):
        parent_index, particle_noise = item
        parent = jnp.take(vorticity, parent_index, axis=0).astype(jnp.float32)
        proposal = PARENT_WEIGHT * jnp.fft.fft2(parent) + NOISE_WEIGHT * spectrum_weight * jnp.fft.fft2(particle_noise.astype(jnp.float32))
        first_rate = tendency(proposal)
        midpoint = proposal + TIME_STEP * first_rate
        final = proposal + (0.5 * TIME_STEP) * (first_rate + tendency(midpoint))
        return jnp.fft.ifft2(final).real.astype(jnp.float32)

    return lax.map(propose_one, (ancestors, noise))
```

```python
import math

import jax
import jax.numpy as jnp
from jax import lax
from jax.sharding import PartitionSpec as P

PARENT_WEIGHT = 0.8
NOISE_WEIGHT = 0.6
VISCOSITY = 0.05
TIME_STEP = 0.1
HIGH = lax.Precision.HIGH


def inner_width():
    return 128


def contract(pattern_text, left_side, right_side):
    return jnp.einsum(pattern_text, left_side, right_side, precision=HIGH)


def outer_table(outer_size, sign_value):
    series = jnp.arange(outer_size, dtype=jnp.int32)
    turn_count = series[:, None] * series[None, :] % outer_size
    angles = 2.0 * math.pi / outer_size * turn_count.astype(jnp.float32)
    cosine = jnp.cos(angles)
    sine = sign_value * jnp.sin(angles)
    first_row = jnp.stack([cosine, -sine], axis=1)
    second_row = jnp.stack([sine, cosine], axis=1)
    return jnp.stack([first_row, second_row], axis=0)


def inner_table(outer_size, inner_size, length, sign_value, twiddle_input):
    outer_index = jnp.arange(outer_size, dtype=jnp.int32)[:, None, None]
    in_index = jnp.arange(inner_size, dtype=jnp.int32)[None, :, None]
    out_index = jnp.arange(inner_size, dtype=jnp.int32)[None, None, :]
    turned_by = in_index if twiddle_input else out_index
    turn_count = (outer_size * in_index * out_index + outer_index * turned_by) % length
    angles = 2.0 * math.pi / length * turn_count.astype(jnp.float32)
    cosine = jnp.cos(angles)
    sine = sign_value * jnp.sin(angles)
    from_real = jnp.stack([cosine, sine], axis=2)
    from_imag = jnp.stack([-sine, cosine], axis=2)
    return jnp.stack([from_real, from_imag], axis=1)


def row_forward(real_part):
    batch_size, row_count, line_length = real_part.shape
    inner_size = inner_width()
    outer_size = line_length // inner_size
    first_table = outer_table(outer_size, -1.0)[:, :, 0, :]
    second_table = inner_table(outer_size, inner_size, line_length, -1.0, True)
    split_rows = real_part.reshape(batch_size, row_count, outer_size, inner_size)
    first = contract("cka,braj->bcrkj", first_table, split_rows)
    second = contract("bdrkj,kdjcl->bcrkl", first, second_table)
    return second.reshape(batch_size, 2, row_count, line_length)


def column_forward(exchanged):
    batch_size, two_parts, line_length, column_count = exchanged.shape
    inner_size = inner_width()
    outer_size = line_length // inner_size
    first_table = outer_table(outer_size, -1.0)
    second_table = inner_table(outer_size, inner_size, line_length, -1.0, True)
    split_cols = exchanged.reshape(batch_size, two_parts, outer_size, inner_size, column_count)
    first = contract("ckda,bdajq->bckjq", first_table, split_cols)
    second = contract("bdkjq,kdjcl->bcqkl", first, second_table)
    return second.reshape(batch_size, two_parts, column_count, line_length)


def column_inverse(spectrum):
    batch_size, two_parts, column_count, line_length = spectrum.shape
    inner_size = inner_width()
    outer_size = line_length // inner_size
    first_table = inner_table(outer_size, inner_size, line_length, 1.0, False)
    second_table = outer_table(outer_size, 1.0)
    split_modes = spectrum.reshape(batch_size, two_parts, column_count, outer_size, inner_size)
    first = contract("bdqkl,kdlcj->bcqkj", split_modes, first_table)
    second = contract("cadk,bdqkj->bcajq", second_table, first)
    return second.reshape(batch_size, two_parts, line_length, column_count)


def row_inverse(exchanged, real_only):
    batch_size, two_parts, row_count, line_length = exchanged.shape
    inner_size = inner_width()
    outer_size = line_length // inner_size
    first_table = inner_table(outer_size, inner_size, line_length, 1.0, False)
    second_table = outer_table(outer_size, 1.0)
    second_table = second_table[:1] if real_only else second_table
    split_modes = exchanged.reshape(batch_size, two_parts, row_count, outer_size, inner_size)
    first = contract("bdrkl,kdlcj->bcrkj", split_modes, first_table)
    second = contract("cadk,bdrkj->cbraj", second_table, first)
    scaling = 1.0 / float(line_length * line_length)
    return second.reshape(-1, batch_size, row_count, line_length) * scaling


def forward_transform(fields):
    rows_spectral = row_forward(fields)
    return column_forward(
        lax.all_to_all(rows_spectral, "field", split_axis=3, concat_axis=2, tiled=True)
    )


def inverse_transform(spectrum, real_only):
    columns_physical = column_inverse(spectrum)
    return row_inverse(
        lax.all_to_all(columns_physical, "field", split_axis=2, concat_axis=3, tiled=True),
        real_only,
    )


def wave_tables(modes, length):
    signed = jnp.where(modes >= length // 2, modes - length, modes)
    wavenumber = 2.0 * math.pi / length * signed.astype(jnp.float32)
    slope = jnp.where(modes == length // 2, jnp.zeros_like(wavenumber), wavenumber)
    retained = jnp.where(3 * jnp.abs(signed) < length, 1.0, 0.0).astype(jnp.float32)
    return (wavenumber, slope, retained)


def layout_tables(line_length, column_count):
    inner_size = inner_width()
    outer_size = line_length // inner_size

    def spectral_order(position):
        return position // inner_size + outer_size * (position % inner_size)

    row_modes = spectral_order(jnp.arange(line_length, dtype=jnp.int32))
    column_modes = spectral_order(
        lax.axis_index("field") * column_count + jnp.arange(column_count, dtype=jnp.int32)
    )
    wave_y, slope_y, kept_y = wave_tables(row_modes, line_length)
    wave_x, slope_x, kept_x = wave_tables(column_modes, line_length)
    squared = wave_x[:, None] ** 2 + wave_y[None, :] ** 2
    inverse_sq = jnp.where(squared > 0, 1.0 / jnp.where(squared > 0, squared, 1.0), 0.0)
    dealias = kept_x[:, None] * kept_y[None, :]
    spectrum_weight = 1.0 / (1.0 + squared)
    return (squared, inverse_sq, dealias, spectrum_weight, slope_x[:, None], slope_y[None, :])


def times_complex(spectral, real_factor, imag_factor):
    real_part = real_factor * spectral[:, 0] - imag_factor * spectral[:, 1]
    imag_part = real_factor * spectral[:, 1] + imag_factor * spectral[:, 0]
    return jnp.stack([real_part, imag_part], axis=1)


def local(vorticity, ancestors, noise):
    particle_count, row_count, line_length = vorticity.shape
    column_count = line_length // lax.axis_size("field")
    first_particle = lax.axis_index("particle") * particle_count
    wanted = lax.dynamic_slice_in_dim(ancestors, first_particle, particle_count)
    shard_rows = lax.all_gather(vorticity, "particle", axis=0, tiled=True)
    labels = jnp.arange(shard_rows.shape[0], dtype=jnp.int32)
    matches = (wanted[:, None] == labels[None, :]).astype(jnp.bfloat16)
    parents = jnp.einsum("pq,qrx->prx", matches, shard_rows, preferred_element_type=jnp.float32)
    squared, inverse_sq, dealias, spectrum_weight, slope_x, slope_y = layout_tables(
        line_length, column_count
    )

    def tendency(spectral):
        potential = spectral * inverse_sq
        spectra = jnp.concatenate(
            [
                times_complex(potential, slope_x, slope_y),
                times_complex(spectral, -slope_y, slope_x),
            ],
            axis=0,
        )
        physical = inverse_transform(spectra, False)
        advection = (
            physical[0, :particle_count] * physical[0, particle_count:]
            + physical[1, :particle_count] * physical[1, particle_count:]
        )
        return -dealias * forward_transform(advection) - VISCOSITY * squared * spectral

    noise_spectra = forward_transform(noise.astype(jnp.float32))
    proposal = (
        PARENT_WEIGHT * forward_transform(parents) + NOISE_WEIGHT * spectrum_weight * noise_spectra
    )
    first_rate = tendency(proposal)
    midpoint = proposal + TIME_STEP * first_rate
    final = proposal + 0.5 * TIME_STEP * (first_rate + tendency(midpoint))
    return inverse_transform(final, True)[0]


def solution(mesh):
    placed = (P("particle", "field", None), P(), P("particle", "field", None))
    return jax.shard_map(
        local, mesh=mesh, in_specs=placed, out_specs=P("particle", "field", None), check_vma=False
    )
```

```python
import math

import jax
import jax.numpy as jnp
import numpy as np
from jax import lax
from jax.sharding import PartitionSpec as P

PARENT_WEIGHT = 0.8
NOISE_WEIGHT = 0.6
VISCOSITY = 0.05
TIME_STEP = 0.1
HIGH = lax.Precision.HIGH


def contract(pattern_text, left_side, right_side):
    return jnp.einsum(pattern_text, left_side, right_side, precision=HIGH)


def wave_numbers(modes, length):
    signed = np.where(modes >= length // 2, modes - length, modes)
    wavenumber = ((2.0 * math.pi / length) * signed).astype(np.float32)
    slope = np.where(modes % length == length // 2, 0.0, wavenumber).astype(np.float32)
    kept = (3 * np.abs(signed) < length).astype(np.float32)
    return wavenumber, slope, kept


def turns(first, second, length):
    angles = 2.0 * math.pi / length * ((first[..., None] * second) % length)
    return np.cos(angles).astype(np.float32), np.sin(angles).astype(np.float32)


def local(vorticity, ancestors, noise):
    particle_count, row_count, length = vorticity.shape
    assert particle_count == 1
    shards = lax.axis_size("field")
    columns = -(-(length // 2 + 1) // shards)
    kept_columns = -(-((length - 1) // 3 + 1) // shards)
    grid = np.arange(length)
    modes = np.arange(shards)[:, None] + shards * np.arange(columns)[None, :]
    cosine, sine = turns(modes, grid, length)
    row_table = np.stack([cosine, -sine], axis=1)
    fold = np.where(modes > length // 2, 0.0, np.where(modes % (length // 2) == 0, 1.0, 2.0))
    fold = (fold / float(length * length)).astype(np.float32)
    row_back = row_table * fold[:, None, :, None]
    column_table = np.stack(turns(grid, grid, length), axis=1)

    own = lax.axis_index("field") + shards * jnp.arange(columns, dtype=jnp.int32)
    wave_x = (2.0 * math.pi / length) * own.astype(jnp.float32)
    slope_x = jnp.where(own >= length // 2, 0.0, wave_x)[:, None]
    kept_x = jnp.where(3 * own < length, 1.0, 0.0)[:, None]
    wave_y, slope_y, kept_y = wave_numbers(grid, length)
    squared = wave_x[:, None] ** 2 + wave_y[None, :] ** 2
    inverse_sq = jnp.where(squared > 0, 1.0 / jnp.where(squared > 0, squared, 1.0), 0.0)
    dealias = kept_x * kept_y[None, :]
    spectrum_weight = 1.0 / (1.0 + squared)
    slope_y = jnp.asarray(slope_y)[None, :]

    def forward(field, width):
        rows = contract("fcnx,rx->fcnr", row_table[:, :, :width], field)
        rows = lax.all_to_all(rows, "field", split_axis=0, concat_axis=0, tiled=True)
        lines = rows.transpose(1, 2, 0, 3).reshape(2, width, length)
        turned = contract("cny,ysm->scnm", lines, column_table)
        return jnp.stack([turned[0, 0] + turned[1, 1], turned[0, 1] - turned[1, 0]])

    def inverse(spectra):
        turned = contract("gcnm,msy->sgcny", spectra, column_table)
        lines = jnp.stack(
            [turned[0, :, 0] - turned[1, :, 1], turned[0, :, 1] + turned[1, :, 0]], axis=1
        )
        lines = lines.reshape(-1, 2, columns, shards, row_count).transpose(3, 0, 1, 2, 4)
        lines = lax.all_to_all(lines, "field", split_axis=0, concat_axis=0, tiled=True)
        return contract("fgcnr,fcnx->grx", lines, row_back)

    def times_imag(spectral, factor):
        return jnp.stack([-factor * spectral[1], factor * spectral[0]])

    def tendency(spectral):
        potential = spectral * inverse_sq
        physical = inverse(
            jnp.stack(
                [
                    times_imag(potential, slope_y),
                    times_imag(potential, -slope_x),
                    times_imag(spectral, slope_x),
                    times_imag(spectral, slope_y),
                ]
            )
        )
        advection = physical[0] * physical[2] + physical[1] * physical[3]
        nonlinear = forward(advection, kept_columns)
        nonlinear = jnp.pad(nonlinear, ((0, 0), (0, columns - kept_columns), (0, 0)))
        return -dealias * nonlinear - VISCOSITY * squared * spectral

    shard_rows = lax.all_gather(vorticity, "particle", axis=0, tiled=True)
    noise_part = NOISE_WEIGHT * spectrum_weight * forward(noise[0].astype(jnp.float32), columns)
    wanted = lax.dynamic_index_in_dim(ancestors, lax.axis_index("particle"), 0, keepdims=False)
    parent = lax.dynamic_index_in_dim(shard_rows, wanted, 0, keepdims=False)
    proposal = PARENT_WEIGHT * forward(parent.astype(jnp.float32), columns) + noise_part
    first_rate = tendency(proposal)
    midpoint = proposal + TIME_STEP * first_rate
    final = proposal + 0.5 * TIME_STEP * (first_rate + tendency(midpoint))
    return inverse(final[None])


def solution(mesh):
    placed = (P("particle", "field", None), P(), P("particle", "field", None))
    return jax.shard_map(
        local, mesh=mesh, in_specs=placed, out_specs=P("particle", "field", None), check_vma=False
    )
```
